32 devices in a mesh: group: 4 (over x, core), dev: 8 (over z, y).
Axes of the slice: x: 2, y: 2, z: 4, core: 2. Of those that a mesh axis runs over, the one named last changes fastest.
Arguments:
- elem_ops: bfloat16 [2048, 48, 64], P(('group', 'dev')), may hold values from -0.75 to 0.75
- elem_stiff: bfloat16 [2048, 48], P(('group', 'dev')), may hold values from 0.5 to 4
- owner: int32 [2048, 1], P(('group', 'dev')), may hold values from 0 to 7; in each aligned block of 64 rows (0 to 63, 64 to 127, ...) at most 16 rows name the same one
- row_slot: int32 [2048], P(('group', 'dev')), may hold values from 0 to 63
- couplings: float32 [2048, 4, 64, 64], P(('group', 'dev')), may hold values from -0.12 to 0.12
- coupling_cols: int32 [2048, 4], P(('group', 'dev')), may hold values from 0 to 191, as said below
- mass: float32 [2048, 64], P(('group', 'dev')), may hold values from 2 to 4
- rhs: float32 [2048, 64], P(('group', 'dev')), may hold values from -48 to 48
Outputs:
- solution: float32 [2048, 64], P(('group', 'dev'))
- residual: float32 [2048, 64], P(('group', 'dev'))
The draws below stay inside these ranges and needn't reach their ends.
Inputs may be any that keep to these rules, and one draw needn't show every extreme that they name: Among the 64 elements of one device (each aligned block of 64 entries) no owner is named more than 16 times, a bound that some block reaches. `coupling_cols`: A value below 64 names a block row of the lower lateral group, one below 128 the device's own, the rest the upper lateral group, as in the operator's step.
All inputs are finite; a program needn't handle non-finite values.
Results may differ from the reference program's by a relative error of at most 0.0005.
Values may be sent and summed in bfloat16 or wider, within the bound.
A program may use at most 64 MiB of HBM per device.

```python
import math
import jax
import jax.numpy as jnp
import numpy as np
from jax import lax

BS = 64
Q = 48
K = 4
ITERS = 3
R = 64
E_DEV = 64
CAP = 16
ELEMS = 2048
ROWS = 2048
N_GROUP = 4
N_DEV = 8


def draw_coupling_cols(key, part):
    region_draw = jax.random.randint(jax.random.fold_in(key, 11), (ROWS, K), 0, 4)
    region = (region_draw + 1) // 2
    within = jax.random.randint(jax.random.fold_in(key, 12), (ROWS, K), 0, R)
    return (region * R + within).astype(jnp.int32)


def place_ends(entries, rng, low, high):
    longest = entries.shape.index(max(entries.shape))
    spots = []
    for shift in (0, 1):
        where = [jax.random.randint(jax.random.fold_in(rng, axis), (), 0, length) for axis, length in enumerate(entries.shape)]
        where[longest] = (where[longest] + shift) % entries.shape[longest]
        spots.append(tuple(where))
    return entries.at[spots[0]].set(low).at[spots[1]].set(high)


def block_levels(key, shape, cuts, low, high):
    gain = 1.0
    for position, blocks in cuts:
        heights = jax.random.uniform(jax.random.fold_in(jax.random.fold_in(key, 6), position), (blocks,), jnp.float32, low / len(cuts), high / len(cuts))
        gain = gain * jnp.repeat(jnp.exp(heights), shape[position] // blocks).reshape((-1,) + (1,) * (len(shape) - 1 - position))
    return gain


def routed_block(stream_key, own, number, rows, amount, top, reach, slope):
    ranking = jax.random.permutation(stream_key, amount)
    heavy_load, ordinary = shares(amount, rows * top, reach, slope, True), shares(amount, rows * top, reach, slope, False)
    places = jnp.arange(amount)

    def named(tallies, offset_by):
        used = int((tallies > 0).sum())
        fixed = max(1, used // 4)
        shifted = fixed + (places - fixed + offset_by * (used - fixed)) % max(1, amount - fixed)
        return jnp.zeros((amount,), jnp.int32).at[ranking[jnp.where(places < fixed, places, shifted)]].set(jnp.asarray(tallies, jnp.int32))

    tallies = jnp.where(number % 4 == 0, named(heavy_load, number // 4), named(ordinary, number - number // 4 - 1))
    mixed = jax.random.permutation(jax.random.fold_in(own, 3), amount)
    source_of, taker = mixed[0:amount // 2 * 2:2], mixed[1:amount // 2 * 2:2]
    margin = jnp.minimum(tallies[source_of] - 1, reach - tallies[taker]) // 2
    margin = jnp.where((source_of == ranking[0]) | (taker == ranking[0]) | (tallies[taker] == 0), 0, jnp.maximum(margin, 0))
    shifted = jax.random.randint(jax.random.fold_in(own, 4), (amount // 2,), 0, 1 << 20) % (margin + 1)
    tallies = tallies.at[source_of].add(-shifted).at[taker].add(shifted)
    items = jnp.searchsorted(jnp.cumsum(tallies), jnp.arange(rows * top), side="right").astype(jnp.int32)
    table = items.reshape(top, rows).T
    table = table[jax.random.permutation(jax.random.fold_in(own, 1), rows)]
    offset_by = jax.random.randint(jax.random.fold_in(own, 2), (rows, 1), 0, top)
    return jnp.take_along_axis(table, (jnp.arange(top)[None, :] + offset_by) % top, axis=1)


def shares(amount, total, bound, slope, full):
    weights = [(1 << 20) // math.isqrt(standing ** slope) + 1 for standing in range(1, amount + 1)]
    largest = bound if full else min(bound, max(-(-total // amount), total * weights[0] // sum(weights)))
    least = 1 if total - largest >= amount - 1 else 0
    counts, rest = [largest] + [least] * (amount - 1), total - largest - least * (amount - 1)
    while rest > 0:
        free = [i for i in range(1, amount) if counts[i] < largest] or [i for i in range(1, amount) if counts[i] < bound]
        pool, left = sum([weights[i] for i in free]), rest
        for i in free:
            extra = min(bound - counts[i], max(1, left * weights[i] // pool), rest)
            counts[i] = counts[i] + extra
            rest = rest - extra
    return np.array(counts)


def scatter_about(own_key, shape, scale, most, shards=(), kind=jnp.bfloat16):
    entries = jax.random.normal(own_key, shape, jnp.float32) * scale
    if len(shards) > 0:
        entries = block_levels(own_key, shape, shards, -0.22, 0.18) * entries
    return jnp.clip(entries, min=-most, max=most).astype(kind)


def setup_inputs(seed: int = 0) -> dict:
    key_of = jax.random.split(jax.random.key(seed), 9)
    elem_ops = scatter_about(key_of[0], (ELEMS, Q, BS), 0.125, 0.75, ((0, 32),))
    elem_stiff = jnp.clip(jnp.exp(math.log(4.0) - 2.0794415 * jax.random.uniform(key_of[1], (ELEMS, Q), jnp.float32) ** block_levels(key_of[1], (ELEMS, Q), ((0, 32),), -0.2, 0.2)), 0.5, 4.0).astype(jnp.bfloat16)
    owner_keys = jax.random.split(jax.random.fold_in(key_of[2], 1), ELEMS // E_DEV)
    owner_turns = jax.random.permutation(jax.random.fold_in(key_of[2], 3), ELEMS // E_DEV)
    owner = jax.vmap(lambda own, number: routed_block(jax.random.fold_in(key_of[2], 2), own, number, E_DEV, N_DEV, 1, CAP, 1))(owner_keys, owner_turns).reshape((ELEMS, 1))
    row_slot = place_ends(jax.random.randint(key_of[3], (ELEMS,), 0, R), jax.random.fold_in(key_of[3], 1), 0, R - 1).astype(jnp.int32)
    couplings = scatter_about(key_of[4], (ROWS, K, BS, BS), 0.02, 0.12, ((0, 32),), jnp.float32)
    coupling_cols = draw_coupling_cols(jax.random.fold_in(key_of[8], 71), 0)
    mass = jnp.clip(jnp.exp(math.log(4.0) - 0.6931472 * jax.random.uniform(key_of[6], (ROWS, BS), jnp.float32) ** block_levels(key_of[6], (ROWS, BS), ((0, 32),), -0.2, 0.2)), 2.0, 4.0)
    rhs = scatter_about(key_of[7], (ROWS, BS), 8.0, 48.0, ((0, 32),), jnp.float32)
    return dict(elem_ops=elem_ops, elem_stiff=elem_stiff, owner=owner, row_slot=row_slot, couplings=couplings, coupling_cols=coupling_cols, mass=mass, rhs=rhs)


def element_tangents(element_ops, element_stiff):
    values = element_ops.astype(jnp.float32)
    weights = element_stiff.astype(jnp.float32)
    return jnp.einsum("eqi,eq,eqj->eij", values, weights, values, precision=lax.Precision.HIGHEST)


def reference(elem_ops, elem_stiff, owner, row_slot, couplings, coupling_cols, mass, rhs):
    blocks = ELEMS // E_DEV
    groups_of = (jnp.arange(blocks, dtype=jnp.int32) // N_DEV).astype(jnp.int32)
    inputs = (elem_ops.reshape(blocks, E_DEV, Q, BS), elem_stiff.reshape(blocks, E_DEV, Q),
              owner.reshape(blocks, E_DEV), row_slot.reshape(blocks, E_DEV), groups_of)

    def add_block(total, pieces):
        block_ops, block_stiff, block_owner, block_slot, group_here = pieces
        target = group_here * (N_DEV * R) + block_owner * R + block_slot
        return total.at[target].add(element_tangents(block_ops, block_stiff)), None

    diag_block, _ = lax.scan(add_block, jnp.zeros((ROWS, BS, BS), jnp.float32), inputs)
    cols_all = coupling_cols.reshape(N_GROUP, N_DEV, R * K)
    row_ids = jnp.arange(ROWS, dtype=jnp.int32)
    group_ids = (row_ids // (N_DEV * R)).astype(jnp.int32)
    dev_ids = ((row_ids // R) % N_DEV).astype(jnp.int32)
    region = (coupling_cols // R).astype(jnp.int32)
    target_group = (group_ids[:, None] + region - 1).astype(jnp.int32)
    valid = (target_group >= 0) & (target_group < N_GROUP)
    target_row = ((target_group * N_DEV + dev_ids[:, None]) * R + coupling_cols % R).astype(jnp.int32)
    target_row = jnp.where(valid, target_row, ROWS).astype(jnp.int32).reshape(-1)

    def apply_operator(field):
        field4 = field.reshape(N_GROUP, N_DEV, R, BS)
        zero = jnp.zeros((1, N_DEV, R, BS), jnp.float32)
        lower = jnp.concatenate([zero, field4[:-1]], axis=0)
        upper = jnp.concatenate([field4[1:], zero], axis=0)
        extended = jnp.stack([lower, field4, upper], axis=2).reshape(N_GROUP, N_DEV, 3 * R, BS)
        nearby = jnp.take_along_axis(extended, cols_all[..., None], axis=2).reshape(ROWS, K, BS)
        own_part = jnp.einsum("rij,rj->ri", diag_block, field, precision=lax.Precision.HIGHEST)
        cross = jnp.einsum("rkij,rkj->ri", couplings, nearby, precision=lax.Precision.HIGHEST)
        returned = jnp.einsum("rkij,ri->rkj", couplings, field, precision=lax.Precision.HIGHEST)
        back = jnp.zeros((ROWS + 1, BS), jnp.float32).at[target_row].add(returned.reshape(ROWS * K, BS))[:ROWS]
        return own_part + mass * field + cross + back

    solution = jnp.zeros_like(rhs)
    residual = rhs
    direction = rhs
    norm_now = jnp.sum(residual * residual)
    for iteration in range(ITERS):
        image = apply_operator(direction)
        alpha = norm_now / jnp.sum(direction * image)
        solution = solution + alpha * direction
        residual = residual - alpha * image
        norm_next = jnp.sum(residual * residual)
        direction = residual + (norm_next / norm_now) * direction
        norm_now = norm_next
    return solution, residual
```

```python
import functools

import jax
import jax.numpy as jnp
from jax import lax
from jax.experimental import pallas as pl
from jax.experimental.pallas import tpu as pltpu
from jax.sharding import PartitionSpec as P

BS = 64
ITERS = 3
SHIFT = 4.0
SCALE = 1.0 / 16.0
MESH = pl.DeviceIdType.MESH
F32 = jnp.float32
BF16 = jnp.bfloat16


def prepare(rows, q, couplings_ref, ops_ref, m_ref, b_ref, wide):
    step = couplings_ref.shape[1]
    ks = couplings_ref.shape[0] // rows
    flat = couplings_ref.reshape(rows * ks * step, BS)
    for i in range(step):
        for k in range(0, ks, 2):
            pair = [flat[pl.ds((k + t) * step + i, rows, stride=ks * step), :] for t in range(2)]
            block = jnp.concatenate(pair, axis=0).T
            m_ref[i * BS : (i + 1) * BS, k * rows : (k + 2) * rows] = block

    @pl.when(pl.program_id(0) == 0)
    def _():
        elems = ops_ref.shape[0]
        wide[...] = ops_ref[...].astype(F32).reshape(elems * q, BS)
        for t in range(q // 2):
            pair = [wide[pl.ds(t + h * (q // 2), elems, stride=q), :] for h in range(2)]
            b_ref[t * BS : (t + 1) * BS, :] = jnp.concatenate(pair, axis=0).T


def pieces(x):
    high = x.astype(BF16)
    rest = x - high.astype(F32)
    mid = rest.astype(BF16)
    low = (rest - mid.astype(F32)).astype(BF16)
    return high, mid, low


def dot(a, b, ca, cb):
    return lax.dot_general(a, b, (((ca,), (cb,)), ((), ())), preferred_element_type=F32)


def pick(x, onehot, axis):
    n = x.shape[0]
    out = dot(jnp.concatenate(pieces(x), axis=0), onehot, 1, axis)
    return out[:n] + out[n : 2 * n] + out[2 * n :]


def pick_rows(onehot, x):
    high, mid, low = pieces(x)
    return dot(onehot, high, 1, 1) + dot(onehot, mid, 1, 1) + dot(onehot, low, 1, 1)


def onehot(condition):
    return jnp.where(condition, 1.0, 0.0).astype(BF16)


def iota(shape, dim):
    return lax.broadcasted_iota(jnp.int32, shape, dim)


def halves(x):
    n = x.shape[0] // 2
    return jnp.concatenate([x[:n], x[n:]], axis=1)


def unhalves(x):
    n = x.shape[1] // 2
    return jnp.concatenate([x[:, :n], x[:, n:]], axis=0)


def kernel(
    n_group, n_dev, cap,
    m_ref, b_ref, stiff_ref, owner_ref, slot_ref, cols_ref, mass_ref, rhs_ref,
    sol_ref, res_ref,
    v_wide, y_part, e_part, w_rows,
    table_src, table_dst, field_src, field_dst, back_src, back_dst,
    near_src, near_dst, sum_src, sum_dst, all_src, all_dst,
    dev_send, dev_recv, near_send, near_recv, all_send, all_recv,
):
    g, d = lax.axis_index("group"), lax.axis_index("dev")
    barrier = pltpu.get_barrier_semaphore()
    for s in range(1, n_dev):
        peer = lax.rem(d + s, n_dev)
        pl.semaphore_signal(barrier, inc=1, device_id=(g, peer), device_id_type=MESH)
    for s in range(1, n_group):
        peer = lax.rem(g + s, n_group)
        pl.semaphore_signal(barrier, inc=1, device_id=(peer, d), device_id_type=MESH)

    elems = owner_ref.shape[1]
    rows = rhs_ref.shape[0]
    slots = n_dev * cap
    pairs = cols_ref.shape[1]
    half = cap // 2

    def to_dev(src, dst, phase):
        copies = []
        for s in range(1, n_dev):
            peer = lax.rem(d + s, n_dev)
            copies.append(pltpu.make_async_remote_copy(
                src_ref=src.at[peer], dst_ref=dst.at[d],
                send_sem=dev_send.at[phase, s - 1], recv_sem=dev_recv.at[phase, s - 1],
                device_id=(g, peer), device_id_type=MESH))
        return copies

    def start(copies):
        for copy in copies:
            copy.start()

    def wait(copies):
        for copy in copies:
            copy.wait()

    owner = owner_ref[...]
    device = iota((n_dev, elems), 0)
    member = device == owner
    ahead = onehot(iota((elems, elems), 0) < iota((elems, elems), 1))
    rank = dot(onehot(member), ahead, 1, 0)
    place = jnp.sum(jnp.where(member, rank + (device * cap).astype(F32), 0.0), axis=0, keepdims=True)
    placed = iota((slots, elems), 0) == place.astype(jnp.int32)
    element_at = onehot(placed)
    named = jnp.sum(jnp.where(placed, (slot_ref[...] + 1).astype(F32), 0.0), axis=1, keepdims=True)
    table_src[...] = jnp.broadcast_to(named - 1.0, (slots, 128)).reshape(n_dev, cap, 128)
    cols = cols_ref[...]
    spot = iota((3 * rows, pairs), 0)
    first = jnp.where(g > 0, 0, rows)
    last = jnp.where(g < n_group - 1, 3 * rows, 2 * rows)
    placer = onehot((spot == cols) & (spot >= first) & (spot < last))
    mass = mass_ref[...].T
    stiff = stiff_ref[...]

    pl.semaphore_wait(barrier, n_dev + n_group - 2)
    table = to_dev(table_src, table_dst, 0)
    start(table)
    table_dst[d] = table_src[d]

    up, down = lax.rem(g + 1, n_group), lax.rem(g + n_group - 1, n_group)

    def to_near(step, kind):
        copies = []
        for side, peer in ((0, up), (1, down)):
            src = near_src.at[step, 0] if kind == 0 else near_src.at[step, 1 + side]
            index = step * 4 + kind * 2 + side
            copies.append(pltpu.make_async_remote_copy(
                src_ref=src, dst_ref=near_dst.at[step, kind * 2 + side],
                send_sem=near_send.at[index], recv_sem=near_recv.at[index],
                device_id=(peer, d), device_id_type=MESH))
        return copies

    def apply(v, step, state):
        near_src[step, 0] = halves(v)
        near_field = to_near(step, 0)
        start(near_field)

        def send_field(requested):
            packed = pick_rows(requested, v).reshape(n_dev, 2, half, BS)
            field_src[step] = jnp.concatenate([packed[:, 0], packed[:, 1]], axis=2)
            copies = to_dev(field_src.at[step], field_dst.at[step], 1 + 2 * step)
            start(copies)
            field_dst[step, d] = field_src[step, d]
            return copies

        requested = state
        if step > 0:
            fields = send_field(requested)
        v_wide[...] = jnp.concatenate([v] * (pairs // rows), axis=1)

        def returned(i, total):
            block = m_ref[pl.ds(pl.multiple_of(i * BS, BS), BS), :]
            return total + block * v_wide[pl.ds(i, 1), :]

        back = lax.fori_loop(0, BS, returned, jnp.zeros((BS, pairs), F32), unroll=8)
        spread = pick(back, placer, 1)
        near_src[step, 1] = halves(spread[:, 2 * rows :])
        near_src[step, 2] = halves(spread[:, :rows])
        near_back = to_near(step, 1)
        start(near_back)
        total = spread[:, rows : 2 * rows] + mass * v
        if step == 0:
            wait(table)
            got = table_dst[...].reshape(slots, 128)[:, :rows].astype(jnp.int32)
            requested = onehot(got == iota((slots, rows), 1))
            fields = send_field(requested)

        wait(fields)
        arrived = field_dst[step]
        arrived = jnp.concatenate([arrived[:, :, :BS], arrived[:, :, BS:]], axis=1)
        ve = pick(arrived.reshape(slots, BS).T, element_at, 0)
        ve = jnp.concatenate([ve, ve], axis=1)
        count = stiff.shape[0]
        lanes = 2 * elems
        for t in range(count):
            product = b_ref[t * BS : (t + 1) * BS, :] * ve
            e_part[t * 8 : (t + 1) * 8, :] = jnp.sum(product.reshape(BS // 8, 8, lanes), axis=0)
        strain = e_part[pl.ds(0, count, stride=8), :]
        for s in range(1, 8):
            strain = strain + e_part[pl.ds(s, count, stride=8), :]
        w_rows[...] = strain * stiff
        ye = jnp.zeros((BS, lanes), F32)
        for t in range(count):
            ye = ye + b_ref[t * BS : (t + 1) * BS, :] * w_rows[t : t + 1, :]
        ye = ye[:, :elems] + ye[:, elems:]
        packed = pick_rows(element_at, ye).reshape(n_dev, 2, half, BS)
        back_src[step] = jnp.concatenate([packed[:, 0], packed[:, 1]], axis=2)
        results = to_dev(back_src.at[step], back_dst.at[step], 2 + 2 * step)
        start(results)
        back_dst[step, d] = back_src[step, d]

        wait(near_field)
        extended = jnp.concatenate(
            [unhalves(near_dst[step, 0]), v, unhalves(near_dst[step, 1])], axis=1)
        nearby = pick(extended, placer, 0)

        def cross(i, carry):
            product = m_ref[pl.ds(pl.multiple_of(i * BS, BS), BS), :] * nearby
            part = jnp.sum(product.reshape(BS // 8, 8, pairs), axis=0)
            for h in range(pairs // 128):
                y_part[h, pl.ds(pl.multiple_of(i * 8, 8), 8), :] = part[:, h * 128 : (h + 1) * 128]
            return carry

        lax.fori_loop(0, BS, cross, 0, unroll=8)
        gathered = jnp.zeros((BS, 128), F32)
        for h in range(pairs // 128):
            for s in range(8):
                gathered = gathered + y_part.at[h][pl.ds(s, BS, stride=8), :]
        for t in range(128 // rows):
            total = total + gathered[:, t * rows : (t + 1) * rows]
        wait(near_back)
        total = total + unhalves(near_dst[step, 2]) + unhalves(near_dst[step, 3])
        wait(results)
        arrived = back_dst[step]
        arrived = jnp.concatenate([arrived[:, :, :BS], arrived[:, :, BS:]], axis=1)
        total = total + pick(arrived.reshape(slots, BS).T, requested, 0)
        return total, requested

    basis = [rhs_ref[...].T]
    requested = None
    for step in range(ITERS):
        image, requested = apply(basis[-1], step, requested)
        basis.append((image - SHIFT * basis[-1]) * SCALE)

    entries = [(a, b) for a in range(ITERS + 1) for b in range(a, ITERS + 1)]
    lane = iota((1, 128), 1)
    sums = jnp.zeros((1, 128), F32)
    for index, (a, b) in enumerate(entries):
        column = jnp.sum(basis[a] * basis[b], axis=0, keepdims=True)
        sums = jnp.where(lane == index, jnp.sum(column, axis=1, keepdims=True), sums)
    for s in range(n_dev):
        sum_src[s] = sums
    partial = to_dev(sum_src, sum_dst, 1 + 2 * ITERS)
    start(partial)
    sum_dst[d] = sums
    wait(partial)
    sums = jnp.sum(sum_dst[...], axis=0)
    all_src[...] = sums
    whole = []
    for s in range(1, n_group):
        peer = lax.rem(g + s, n_group)
        whole.append(pltpu.make_async_remote_copy(
            src_ref=all_src, dst_ref=all_dst.at[g],
            send_sem=all_send.at[s - 1], recv_sem=all_recv.at[s - 1],
            device_id=(peer, d), device_id_type=MESH))
    start(whole)
    all_dst[g] = sums
    wait(whole)
    sums = jnp.sum(all_dst[...], axis=0)
    gram = {}
    for index, (a, b) in enumerate(entries):
        value = jnp.broadcast_to(sums[:, index : index + 1], (1, rows))
        gram[a, b] = gram[b, a] = value

    def inner(a, b):
        out = None
        for i, x in enumerate(a):
            line = None
            for j, y in enumerate(b):
                term = y * gram[i, j]
                line = term if line is None else line + term
            out = x * line if out is None else out + x * line
        return out

    def image_of(c):
        out = [SHIFT * x for x in c] + [jnp.zeros_like(c[0])]
        return [out[0]] + [out[k + 1] + c[k] * (1.0 / SCALE) for k in range(len(c))]

    def combine(a, scale, b):
        size = max(len(a), len(b))
        out = []
        for k in range(size):
            if k >= len(b):
                out.append(a[k])
            elif k >= len(a):
                out.append(scale * b[k])
            else:
                out.append(a[k] + scale * b[k])
        return out

    one = jnp.ones((1, rows), F32)
    answer, residual, direction = [], [one], [one]
    norm = gram[0, 0]
    for step in range(ITERS):
        image = image_of(direction)
        alpha = norm / inner(direction, image)
        answer = combine(answer, alpha, direction)
        residual = combine(residual, -alpha, image)
        if step + 1 < ITERS:
            following = inner(residual, residual)
            direction = combine(residual, following / norm, direction)
            norm = following
    sol_ref[...] = sum(c * w for c, w in zip(answer, basis)).T
    res_ref[...] = sum(c * w for c, w in zip(residual, basis)).T


def per_device(n_group, n_dev, elem_ops, elem_stiff, owner, row_slot, couplings, coupling_cols, mass, rhs):
    rows, ks = coupling_cols.shape
    elems, q, _ = elem_ops.shape
    pairs = rows * ks
    cap = max(16, 2 * elems // n_dev)
    slots = n_dev * cap
    steps = 8
    per = BS // steps
    m, b = pl.pallas_call(
        functools.partial(prepare, rows, q),
        grid=(steps,),
        in_specs=[
            pl.BlockSpec((pairs, per, BS), lambda i: (0, i, 0)),
            pl.BlockSpec((elems, q, BS), lambda i: (0, 0, 0)),
        ],
        out_specs=[
            pl.BlockSpec((per * BS, pairs), lambda i: (i, 0)),
            pl.BlockSpec((q // 2 * BS, 2 * elems), lambda i: (0, 0)),
        ],
        out_shape=[
            jax.ShapeDtypeStruct((BS * BS, pairs), F32),
            jax.ShapeDtypeStruct((q // 2 * BS, 2 * elems), F32),
        ],
        scratch_shapes=[pltpu.VMEM((elems * q, BS), F32)],
        compiler_params=pltpu.CompilerParams(vmem_limit_bytes=24 * 2**20),
    )(couplings.reshape(pairs, BS, BS), elem_ops)
    stiff = elem_stiff.T.astype(F32)
    stiff = jnp.concatenate([stiff[: q // 2], stiff[q // 2 :]], axis=1)
    phases = 2 + 2 * ITERS
    vmem = pl.BlockSpec(memory_space=pltpu.VMEM)
    packet = (n_dev, cap // 2, 2 * BS)
    return pl.pallas_call(
        functools.partial(kernel, n_group, n_dev, cap),
        in_specs=[vmem] * 8,
        out_specs=[vmem] * 2,
        out_shape=[jax.ShapeDtypeStruct(rhs.shape, F32)] * 2,
        scratch_shapes=[
            pltpu.VMEM((BS, pairs), F32),
            pltpu.VMEM((pairs // 128, BS * 8, 128), F32),
            pltpu.VMEM((q // 2 * 8, 2 * elems), F32),
            pltpu.VMEM((q // 2, 2 * elems), F32),
            pltpu.VMEM((n_dev, cap, 128), F32),
            pltpu.VMEM((n_dev, cap, 128), F32),
            pltpu.VMEM((ITERS,) + packet, F32),
            pltpu.VMEM((ITERS,) + packet, F32),
            pltpu.VMEM((ITERS,) + packet, F32),
            pltpu.VMEM((ITERS,) + packet, F32),
            pltpu.VMEM((ITERS, 3, BS // 2, 2 * rows), F32),
            pltpu.VMEM((ITERS, 4, BS // 2, 2 * rows), F32),
            pltpu.VMEM((n_dev, 1, 128), F32),
            pltpu.VMEM((n_dev, 1, 128), F32),
            pltpu.VMEM((1, 128), F32),
            pltpu.VMEM((n_group, 1, 128), F32),
            pltpu.SemaphoreType.DMA((phases, n_dev - 1)),
            pltpu.SemaphoreType.DMA((phases, n_dev - 1)),
            pltpu.SemaphoreType.DMA((4 * ITERS,)),
            pltpu.SemaphoreType.DMA((4 * ITERS,)),
            pltpu.SemaphoreType.DMA((n_group - 1,)),
            pltpu.SemaphoreType.DMA((n_group - 1,)),
        ],
        compiler_params=pltpu.CompilerParams(
            collective_id=0, has_side_effects=True, vmem_limit_bytes=32 * 2**20),
    )(m, b, stiff, owner.reshape(1, elems), row_slot.reshape(1, elems),
      coupling_cols.T.reshape(1, pairs), mass, rhs)


def solution(mesh):
    both = ("group", "dev")
    placed = (
        P(both, None, None), P(both, None), P(both, None), P(both),
        P(both, None, None, None), P(both, None), P(both, None), P(both, None),
    )
    return jax.shard_map(
        functools.partial(per_device, mesh.shape["group"], mesh.shape["dev"]),
        mesh=mesh,
        in_specs=placed,
        out_specs=(P(both, None), P(both, None)),
        check_vma=False,
    )
```

```python
import functools

import jax
import jax.numpy as jnp
from jax import lax
from jax.experimental import pallas as pl
from jax.experimental.pallas import tpu as pltpu
from jax.sharding import PartitionSpec as P

BS = 64
ITERS = 3
SHIFT = 4.0
SCALE = 1.0 / 16.0
MESH = pl.DeviceIdType.MESH
F32 = jnp.float32
BF16 = jnp.bfloat16


def pieces(x):
    high = x.astype(BF16)
    rest = x - high.astype(F32)
    mid = rest.astype(BF16)
    low = (rest - mid.astype(F32)).astype(BF16)
    return high, mid, low


def dot(a, b, ca, cb):
    return lax.dot_general(a, b, (((ca,), (cb,)), ((), ())), preferred_element_type=F32)


def pick(x, onehot, axis):
    n = x.shape[0]
    out = dot(jnp.concatenate(pieces(x), axis=0), onehot, 1, axis)
    return out[:n] + out[n : 2 * n] + out[2 * n :]


def onehot(condition):
    return jnp.where(condition, 1.0, 0.0).astype(BF16)


def iota(shape, dim):
    return lax.broadcasted_iota(jnp.int32, shape, dim)


def halves(x):
    n = x.shape[0] // 2
    return jnp.concatenate([x[:n], x[n:]], axis=1)


def unhalves(x):
    n = x.shape[1] // 2
    return jnp.concatenate([x[:, :n], x[:, n:]], axis=0)


def kernel(
    n_group, n_dev, cap,
    couplings_ref, ops_ref, stiff_ref, owner_ref, slot_ref, cols_ref, mass_ref, rhs_ref,
    sol_ref, res_ref,
    raw, ops, wide, m_ref, b_ref, v_wide, y_part, e_part, w_rows,
    table_src, table_dst, elem_src, elem_dst,
    near_src, near_dst, sum_src, sum_dst, all_src, all_dst,
    load_sem, dev_send, dev_recv, near_send, near_recv, all_send, all_recv,
):
    g, d = lax.axis_index("group"), lax.axis_index("dev")
    load_ops = pltpu.make_async_copy(ops_ref, ops, load_sem.at[0])
    load_raw = pltpu.make_async_copy(couplings_ref, raw, load_sem.at[1])
    load_ops.start()
    load_raw.start()
    barrier = pltpu.get_barrier_semaphore()
    for s in range(1, n_dev):
        peer = lax.rem(d + s, n_dev)
        pl.semaphore_signal(barrier, inc=1, device_id=(g, peer), device_id_type=MESH)
    for s in range(1, n_group):
        peer = lax.rem(g + s, n_group)
        pl.semaphore_signal(barrier, inc=1, device_id=(peer, d), device_id_type=MESH)

    elems = owner_ref.shape[1]
    rows = rhs_ref.shape[0]
    slots = n_dev * cap
    ks = cols_ref.shape[0]
    pairs = rows * ks
    q = stiff_ref.shape[0]

    def to_dev(src, dst, phase):
        copies = []
        for s in range(1, n_dev):
            peer = lax.rem(d + s, n_dev)
            copies.append(pltpu.make_async_remote_copy(
                src_ref=src.at[peer], dst_ref=dst.at[d],
                send_sem=dev_send.at[phase, s - 1], recv_sem=dev_recv.at[phase, s - 1],
                device_id=(g, peer), device_id_type=MESH))
        return copies

    def start(copies):
        for copy in copies:
            copy.start()

    def wait(copies):
        for copy in copies:
            copy.wait()

    device = iota((n_dev, elems), 0)
    member = device == owner_ref[...]
    ahead = onehot(iota((elems, elems), 0) < iota((elems, elems), 1))
    rank = dot(onehot(member), ahead, 1, 0)
    place = jnp.sum(jnp.where(member, rank + (device * cap).astype(F32), 0.0), axis=0, keepdims=True)
    placed = iota((slots, elems), 0) == place.astype(jnp.int32)
    element_at = onehot(placed)
    named = jnp.sum(jnp.where(placed, (slot_ref[...] + 1).astype(F32), 0.0), axis=1, keepdims=True)
    stiff = dot(element_at, stiff_ref[...], 1, 1)
    stiff = jnp.concatenate([stiff, jnp.zeros((slots, BS - q), F32)], axis=1)
    sheet = jnp.concatenate([stiff, jnp.broadcast_to(named - 1.0, (slots, BS))], axis=1)
    table_src[...] = sheet.reshape(n_dev, cap, 2 * BS)
    load_ops.wait()
    wide[...] = ops[...].astype(F32).reshape(elems * q, BS)
    for t in range(q // 2):
        pair = [wide[pl.ds(t + h * (q // 2), elems, stride=q), :] for h in range(2)]
        moved = dot(element_at, jnp.concatenate(pair, axis=1).astype(BF16), 1, 0)
        elem_src[:, t * cap : (t + 1) * cap, :] = moved.reshape(n_dev, cap, 2 * BS).astype(BF16)

    pl.semaphore_wait(barrier, n_dev + n_group - 2)
    table = to_dev(table_src, table_dst, 0)
    start(table)
    elements = to_dev(elem_src, elem_dst, 1)
    start(elements)
    table_dst[d] = table_src[d]
    elem_dst[d] = elem_src[d]

    cols = jnp.concatenate([cols_ref[k : k + 1, :] for k in range(ks)], axis=1)
    spot = iota((3 * rows, pairs), 0)
    first = jnp.where(g > 0, 0, rows)
    last = jnp.where(g < n_group - 1, 3 * rows, 2 * rows)
    placer = onehot((spot == cols) & (spot >= first) & (spot < last))
    mass = mass_ref[...].T

    up, down = lax.rem(g + 1, n_group), lax.rem(g + n_group - 1, n_group)

    def to_near(step, kind):
        copies = []
        for side, peer in ((0, up), (1, down)):
            src = near_src.at[step, 0] if kind == 0 else near_src.at[step, 1 + side]
            index = step * 4 + kind * 2 + side
            copies.append(pltpu.make_async_remote_copy(
                src_ref=src, dst_ref=near_dst.at[step, kind * 2 + side],
                send_sem=near_send.at[index], recv_sem=near_recv.at[index],
                device_id=(peer, d), device_id_type=MESH))
        return copies

    def transpose_couplings():
        load_raw.wait()

        def one(i, carry):
            for k in range(0, ks, 2):
                pair = [raw[pl.ds((k + t) * BS + i, rows, stride=ks * BS), :] for t in range(2)]
                block = jnp.concatenate(pair, axis=0).T
                m_ref[pl.ds(pl.multiple_of(i * BS, BS), BS), k * rows : (k + 2) * rows] = block
            return carry

        lax.fori_loop(0, BS, one, 0, unroll=4)

    def take_elements():
        wait(table)
        wait(elements)
        sheet = table_dst[...].reshape(slots, 2 * BS)
        held = onehot(sheet[:, BS:].astype(jnp.int32) == iota((slots, rows), 1))
        for t in range(q // 2):
            block = elem_dst[:, t * cap : (t + 1) * cap, :].astype(F32).reshape(slots, 2 * BS).T
            b_ref[t * BS : (t + 1) * BS, :] = block[:BS]
            b_ref[(t + q // 2) * BS : (t + q // 2 + 1) * BS, :] = block[BS:]
        return held, sheet.T[:q]

    def apply_elements(v, held, stiff):
        ve = pick(v, held, 1)
        for t in range(q):
            product = b_ref[t * BS : (t + 1) * BS, :] * ve
            part = jnp.sum(product.reshape(BS // 8, 8, slots), axis=0)
            for h in range(slots // 128):
                e_part[h, t * 8 : (t + 1) * 8, :] = part[:, h * 128 : (h + 1) * 128]
        for h in range(slots // 128):
            strain = e_part.at[h][pl.ds(0, q, stride=8), :]
            for s in range(1, 8):
                strain = strain + e_part.at[h][pl.ds(s, q, stride=8), :]
            w_rows[:, h * 128 : (h + 1) * 128] = strain * stiff[:, h * 128 : (h + 1) * 128]
        ye = jnp.zeros((BS, slots), F32)
        for t in range(q):
            ye = ye + b_ref[t * BS : (t + 1) * BS, :] * w_rows[t : t + 1, :]
        return pick(ye, held, 0)

    def apply(v, step, state):
        near_src[step, 0] = halves(v)
        near_field = to_near(step, 0)
        start(near_field)
        v_wide[...] = jnp.concatenate([v] * ks, axis=1)
        if step == 0:
            transpose_couplings()

        def returned(i, total):
            block = m_ref[pl.ds(pl.multiple_of(i * BS, BS), BS), :]
            return total + block * v_wide[pl.ds(i, 1), :]

        back = lax.fori_loop(0, BS, returned, jnp.zeros((BS, pairs), F32), unroll=8)
        spread = pick(back, placer, 1)
        near_src[step, 1] = halves(spread[:, 2 * rows :])
        near_src[step, 2] = halves(spread[:, :rows])
        near_back = to_near(step, 1)
        start(near_back)
        total = spread[:, rows : 2 * rows] + mass * v
        if step > 0:
            total = total + apply_elements(v, *state)

        wait(near_field)
        extended = jnp.concatenate(
            [unhalves(near_dst[step, 0]), v, unhalves(near_dst[step, 1])], axis=1)
        nearby = pick(extended, placer, 0)

        def cross(i, carry):
            product = m_ref[pl.ds(pl.multiple_of(i * BS, BS), BS), :] * nearby
            part = jnp.sum(product.reshape(BS // 8, 8, pairs), axis=0)
            for h in range(pairs // 128):
                y_part[h, pl.ds(pl.multiple_of(i * 8, 8), 8), :] = part[:, h * 128 : (h + 1) * 128]
            return carry

        lax.fori_loop(0, BS, cross, 0, unroll=8)
        gathered = jnp.zeros((BS, 128), F32)
        for h in range(pairs // 128):
            for s in range(8):
                gathered = gathered + y_part.at[h][pl.ds(s, BS, stride=8), :]
        for t in range(128 // rows):
            total = total + gathered[:, t * rows : (t + 1) * rows]
        if step == 0:
            state = take_elements()
            total = total + apply_elements(v, *state)
        wait(near_back)
        total = total + unhalves(near_dst[step, 2]) + unhalves(near_dst[step, 3])
        return total, state

    basis = [rhs_ref[...].T]
    state = None
    for step in range(ITERS):
        image, state = apply(basis[-1], step, state)
        basis.append((image - SHIFT * basis[-1]) * SCALE)

    entries = [(a, b) for a in range(ITERS + 1) for b in range(a, ITERS + 1)]
    lane = iota((1, 128), 1)
    sums = jnp.zeros((1, 128), F32)
    for index, (a, b) in enumerate(entries):
        column = jnp.sum(basis[a] * basis[b], axis=0, keepdims=True)
        sums = jnp.where(lane == index, jnp.sum(column, axis=1, keepdims=True), sums)
    for s in range(n_dev):
        sum_src[s] = sums
    partial = to_dev(sum_src, sum_dst, 2)
    start(partial)
    sum_dst[d] = sums
    wait(partial)
    sums = jnp.sum(sum_dst[...], axis=0)
    all_src[...] = sums
    whole = []
    for s in range(1, n_group):
        peer = lax.rem(g + s, n_group)
        whole.append(pltpu.make_async_remote_copy(
            src_ref=all_src, dst_ref=all_dst.at[g],
            send_sem=all_send.at[s - 1], recv_sem=all_recv.at[s - 1],
            device_id=(peer, d), device_id_type=MESH))
    start(whole)
    all_dst[g] = sums
    wait(whole)
    sums = jnp.sum(all_dst[...], axis=0)
    gram = {}
    for index, (a, b) in enumerate(entries):
        value = jnp.broadcast_to(sums[:, index : index + 1], (1, rows))
        gram[a, b] = gram[b, a] = value

    def inner(a, b):
        out = None
        for i, x in enumerate(a):
            line = None
            for j, y in enumerate(b):
                term = y * gram[i, j]
                line = term if line is None else line + term
            out = x * line if out is None else out + x * line
        return out

    def image_of(c):
        out = [SHIFT * x for x in c] + [jnp.zeros_like(c[0])]
        return [out[0]] + [out[k + 1] + c[k] * (1.0 / SCALE) for k in range(len(c))]

    def combine(a, scale, b):
        size = max(len(a), len(b))
        out = []
        for k in range(size):
            if k >= len(b):
                out.append(a[k])
            elif k >= len(a):
                out.append(scale * b[k])
            else:
                out.append(a[k] + scale * b[k])
        return out

    one = jnp.ones((1, rows), F32)
    answer, residual, direction = [], [one], [one]
    norm = gram[0, 0]
    for step in range(ITERS):
        image = image_of(direction)
        alpha = norm / inner(direction, image)
        answer = combine(answer, alpha, direction)
        residual = combine(residual, -alpha, image)
        if step + 1 < ITERS:
            following = inner(residual, residual)
            direction = combine(residual, following / norm, direction)
            norm = following
    sol_ref[...] = sum(c * w for c, w in zip(answer, basis)).T
    res_ref[...] = sum(c * w for c, w in zip(residual, basis)).T


def per_device(n_group, n_dev, elem_ops, elem_stiff, owner, row_slot, couplings, coupling_cols, mass, rhs):
    rows, ks = coupling_cols.shape
    elems, q, _ = elem_ops.shape
    pairs = rows * ks
    cap = max(16, 2 * elems // n_dev)
    slots = n_dev * cap
    vmem = pl.BlockSpec(memory_space=pltpu.VMEM)
    anywhere = pl.BlockSpec(memory_space=pl.ANY)
    packet = (n_dev, q // 2 * cap, 2 * BS)
    return pl.pallas_call(
        functools.partial(kernel, n_group, n_dev, cap),
        in_specs=[anywhere] * 2 + [vmem] * 6,
        out_specs=[vmem] * 2,
        out_shape=[jax.ShapeDtypeStruct(rhs.shape, F32)] * 2,
        scratch_shapes=[
            pltpu.VMEM((pairs * BS, BS), F32),
            pltpu.VMEM((elems, q, BS), BF16),
            pltpu.VMEM((elems * q, BS), F32),
            pltpu.VMEM((BS * BS, pairs), F32),
            pltpu.VMEM((q * BS, slots), F32),
            pltpu.VMEM((BS, pairs), F32),
            pltpu.VMEM((pairs // 128, BS * 8, 128), F32),
            pltpu.VMEM((slots // 128, q * 8, 128), F32),
            pltpu.VMEM((q, slots), F32),
            pltpu.VMEM((n_dev, cap, 2 * BS), F32),
            pltpu.VMEM((n_dev, cap, 2 * BS), F32),
            pltpu.VMEM(packet, BF16),
            pltpu.VMEM(packet, BF16),
            pltpu.VMEM((ITERS, 3, BS // 2, 2 * rows), F32),
            pltpu.VMEM((ITERS, 4, BS // 2, 2 * rows), F32),
            pltpu.VMEM((n_dev, 1, 128), F32),
            pltpu.VMEM((n_dev, 1, 128), F32),
            pltpu.VMEM((1, 128), F32),
            pltpu.VMEM((n_group, 1, 128), F32),
            pltpu.SemaphoreType.DMA((2,)),
            pltpu.SemaphoreType.DMA((3, n_dev - 1)),
            pltpu.SemaphoreType.DMA((3, n_dev - 1)),
            pltpu.SemaphoreType.DMA((4 * ITERS,)),
            pltpu.SemaphoreType.DMA((4 * ITERS,)),
            pltpu.SemaphoreType.DMA((n_group - 1,)),
            pltpu.SemaphoreType.DMA((n_group - 1,)),
        ],
        compiler_params=pltpu.CompilerParams(
            collective_id=0, has_side_effects=True, vmem_limit_bytes=56 * 2**20),
    )(couplings.reshape(pairs * BS, BS), elem_ops, elem_stiff.T, owner.reshape(1, elems),
      row_slot.reshape(1, elems), coupling_cols.T, mass, rhs)


def solution(mesh):
    both = ("group", "dev")
    placed = (
        P(both, None, None), P(both, None), P(both, None), P(both),
        P(both, None, None, None), P(both, None), P(both, None), P(both, None),
    )
    return jax.shard_map(
        functools.partial(per_device, mesh.shape["group"], mesh.shape["dev"]),
        mesh=mesh,
        in_specs=placed,
        out_specs=(P(both, None), P(both, None)),
        check_vma=False,
    )
```
